128 devices in a mesh: section: 2 (over core), row: 4 (over y), col: 16 (over x, z).
Axes of the slice: x: 4, y: 4, z: 4, core: 2. Of those that a mesh axis runs over, the one named last changes fastest.
Arguments:
- activations: bfloat16 [32768, 4096], P(('section', 'col'), 'row'), parts along dimension 0, may hold values from -300 to 300
- out_grads: bfloat16 [2, 32768, 4096], P(None, ('section', 'col')), parts along dimension 1, may hold values from -0.25 to 0.25
- weights: float32 [4, 4096, 4096], P('section', 'col', 'row'), parts along dimension 0, may hold values from -125 to 125
- row_prev: float32 [4, 4096], P('section', 'col'), parts along dimension 0, may hold values from 0.002 to 16
- col_prev: float32 [4, 4096], P('section', 'row'), parts along dimension 0, may hold values from 0.002 to 16
Outputs:
- new_weights: float32 [4, 4096, 4096], P('section', 'col', 'row'), parts along dimension 0
- direction: bfloat16 [4, 4096, 4096], P('section', 'col', 'row'), parts along dimension 0
- row_factor: float32 [4, 4096], P('section', 'col'), parts along dimension 0
- col_factor: float32 [4, 4096], P('section', 'row'), parts along dimension 0
- update_rms: float32 [4], P('section'), parts along dimension 0
- param_rms: float32 [4], P('section'), parts along dimension 0
The draws below stay inside these ranges and needn't reach their ends.
There are 2 independent parts, one for each index of `section`. The reference program is written for one: setup_inputs(seed, part) draws one part's arguments, and reference() takes and returns one part's arrays. A program takes and returns all parts, laid end to end along the dimension named above; each array names one. Nothing has to cross between parts.
All inputs are finite; a program needn't handle non-finite values.
Results may differ from the reference program's by a relative error of at most 0.019.
Values may be sent and summed in bfloat16 or wider, within the bound.
No kernel may reach another device: no remote copies, remote signals or barrier semaphores. Data moves between devices by JAX's collectives and lax.ppermute only.
A program may use at most 128 MiB of HBM per device.

```python
import math
import jax
import jax.numpy as jnp
from jax import lax

D = 4096
INNER = 4096
MATS = 2
TOK_DEV = 1024
TOKENS = 16384
N_COL = 16


def token_topics(key):
    key = jax.random.fold_in(key, 101)
    ticket = jax.random.randint(key, (TOKENS,), 0, 100)
    return (ticket >= 4).astype(jnp.int32) + (ticket >= 16).astype(jnp.int32) + (ticket >= 46).astype(jnp.int32)


def topic_weight(topic):
    share = jnp.where(topic == 0, 0.04, jnp.where(topic == 1, 0.12, jnp.where(topic == 2, 0.3, 0.54)))
    return 1.0 + 99.0 * share


def grad_features(key):
    key = jax.random.fold_in(key, 102)
    first, second = jax.random.split(key, 2)
    rising = 3.0 ** (jnp.arange(INNER, dtype=jnp.float32) / INNER)
    spread = jnp.exp(jax.random.uniform(first, (MATS, INNER), minval=0.0, maxval=math.log(4.0)))
    groups = jax.random.randint(second, (MATS, INNER // 16), 0, 4)
    return (rising[None, :] * spread, jnp.repeat(groups, 16, axis=1))


def input_features(key):
    key = jax.random.fold_in(key, 103)
    first, second = jax.random.split(key, 2)
    rising = 3.0 ** (jnp.arange(D, dtype=jnp.float32) / D)
    spread = jnp.exp(jax.random.uniform(first, (D,), minval=0.0, maxval=math.log(4.0)))
    groups = jax.random.randint(second, (D // 16,), 0, 4)
    return (rising * spread, jnp.repeat(groups, 16, axis=0))


def draw_activations(key, part):
    topics = token_topics(key)
    amplitude, feature_topic = input_features(key)
    key = jax.random.fold_in(key, 11)
    first, second = jax.random.split(key, 2)
    blocks = jnp.exp(jax.random.uniform(second, (TOKENS // TOK_DEV, D // 16), minval=math.log(0.5), maxval=math.log(2.0)))
    block_scale = jnp.repeat(jnp.repeat(blocks, TOK_DEV, axis=0), 16, axis=1)
    boost = 1.0 + 9.0 * (topics[:, None] == feature_topic[None, :]).astype(jnp.float32)
    base = jnp.clip(jax.random.normal(first, (TOKENS, D)), -5.0, 5.0)
    return (base * amplitude[None, :] * block_scale * boost * 0.25).astype(jnp.bfloat16)


def draw_out_grads(key, part):
    topics = token_topics(key)
    amplitude, feature_topic = grad_features(key)
    key = jax.random.fold_in(key, 12)
    first, second = jax.random.split(key, 2)
    blocks = jnp.exp(jax.random.uniform(second, (MATS, TOKENS // TOK_DEV, INNER // 16), minval=math.log(0.5), maxval=math.log(2.0)))
    block_scale = jnp.repeat(jnp.repeat(blocks, TOK_DEV, axis=1), 16, axis=2)
    boost = 1.0 + 9.0 * (topics[None, :, None] == feature_topic[:, None, :]).astype(jnp.float32)
    base = jnp.clip(jax.random.normal(first, (MATS, TOKENS, INNER)), -5.0, 5.0)
    factor = 0.026 / math.sqrt(TOKENS)
    return (base * amplitude[:, None, :] * block_scale * boost * factor).astype(jnp.bfloat16)


def draw_weights(key, part):
    key = jax.random.fold_in(key, 13)
    first, second = jax.random.split(key, 2)
    rows = jnp.arange(INNER, dtype=jnp.float32)[:, None]
    columns = jnp.arange(D, dtype=jnp.float32)[None, :]
    rising = 3.0 ** (rows / INNER + columns / D) * 0.5
    spread = jnp.exp(jax.random.uniform(second, (MATS, INNER, 1), minval=0.0, maxval=math.log(4.0)))
    base = jnp.clip(jax.random.normal(first, (MATS, INNER, D)), -5.0, 5.0)
    return (base * rising * spread).astype(jnp.float32)


def draw_row_prev(key, part):
    amplitude, feature_topic = grad_features(key)
    key = jax.random.fold_in(key, 14)
    noise = jnp.exp(jax.random.uniform(key, (MATS, INNER), minval=math.log(0.5), maxval=math.log(2.0)))
    return (0.001 * amplitude * amplitude * topic_weight(feature_topic) * noise).astype(jnp.float32)


def draw_col_prev(key, part):
    amplitude, feature_topic = input_features(key)
    key = jax.random.fold_in(key, 15)
    noise = jnp.exp(jax.random.uniform(key, (MATS, D), minval=math.log(0.5), maxval=math.log(2.0)))
    profile = amplitude * amplitude * topic_weight(feature_topic)
    return (0.001 * profile[None, :] * noise).astype(jnp.float32)


def setup_inputs(seed: int = 0, part: int = 0) -> dict:
    keys = jax.random.split(jax.random.key(seed), 6)
    own_keys = jax.random.split(jax.random.fold_in(keys[5], part), 6)
    return {
        "activations": draw_activations(jax.random.fold_in(jax.random.fold_in(keys[5], part), 71), part),
        "out_grads": draw_out_grads(jax.random.fold_in(jax.random.fold_in(keys[5], part), 71), part),
        "weights": draw_weights(jax.random.fold_in(jax.random.fold_in(keys[5], part), 71), part),
        "row_prev": draw_row_prev(jax.random.fold_in(jax.random.fold_in(keys[5], part), 71), part),
        "col_prev": draw_col_prev(jax.random.fold_in(jax.random.fold_in(keys[5], part), 71), part),
    }


decay_rate = 1.0 - 100.0 ** (-0.8)
square_eps = 1e-30
step_scale = 0.01
clip_limit = 1.0

def reference(activations, out_grads, weights, row_prev, col_prev):
    blocks_x = activations.reshape(N_COL, TOK_DEV, D)
    updated = []
    directions = []
    row_list = []
    col_list = []
    update_list = []
    param_list = []
    for number in range(MATS):
        blocks_dy = out_grads[number].reshape(N_COL, TOK_DEV, INNER)

        def add_block(running, pair):
            x_block, dy_block = pair
            term = lax.dot_general(dy_block, x_block, (((0,), (0,)), ((), ())), preferred_element_type=jnp.float32)
            term = lax.optimization_barrier(term.astype(jnp.bfloat16))
            return (running + term.astype(jnp.float32), None)
        gradient, _ = lax.scan(add_block, jnp.zeros((INNER, D), jnp.float32), (blocks_x, blocks_dy))
        square = gradient * gradient + square_eps
        row_new = decay_rate * row_prev[number] + (1.0 - decay_rate) * lax.optimization_barrier(jnp.sum(square, axis=1)) / D
        col_new = decay_rate * col_prev[number] + (1.0 - decay_rate) * lax.optimization_barrier(jnp.sum(square, axis=0)) / INNER
        row_mean = jnp.sum(row_new) / INNER
        scaled = gradient / jnp.sqrt(row_new[:, None] * col_new[None, :] / row_mean)
        update_scale = jnp.sqrt(jnp.sum(scaled * scaled) / (INNER * D) + 1e-06)
        clipped = scaled / jnp.maximum(1.0, update_scale / clip_limit)
        param_scale = jnp.sqrt(jnp.sum(weights[number] * weights[number]) / (INNER * D) + 1e-06)
        updated.append(weights[number] - step_scale * param_scale * clipped)
        directions.append(clipped.astype(jnp.bfloat16))
        row_list.append(row_new)
        col_list.append(col_new)
        update_list.append(update_scale)
        param_list.append(param_scale)
    return (jnp.stack(updated), jnp.stack(directions), jnp.stack(row_list), jnp.stack(col_list), jnp.stack(update_list), jnp.stack(param_list))
```

```python
import functools

import jax
import jax.numpy as jnp
from jax import lax
from jax.experimental import pallas as pl
from jax.experimental.pallas import tpu as pltpu
from jax.sharding import PartitionSpec as P

D = 4096
INNER = 4096
SIDE = 4
TILE = 256

decay_rate = 1.0 - 100.0 ** (-0.8)
square_eps = 1e-30
step_scale = 0.01
clip_limit = 1.0
f32 = jnp.float32
bf16 = jnp.bfloat16


def multiply(blocks, x_ref, targets):
    for part, block in enumerate(blocks):
        term = lax.dot_general(
            block[0], x_ref[...], (((0,), (0,)), ((), ())), preferred_element_type=f32
        ).astype(bf16)
        targets[0][part, 0] = term[:, :TILE]
        targets[1][part, 0] = term[:, TILE:]


def product_kernel(count, here, d0, d1, d2, d3, x_ref, *targets):
    if count == 1:
        multiply((d0, d1, d2, d3), x_ref, targets)
        return
    for chunk in range(count):

        @pl.when(pl.program_id(0) == chunk)
        def _():
            multiply((d0, d1, d2, d3), x_ref, targets[2 * chunk : 2 * chunk + 2])


def products(here, out_grads, activations, axis, offsets):
    count = len(offsets)
    mats, tokens, _ = out_grads.shape

    def block_spec(part):
        def index(c, m, t):
            along = t[0] >> 2 if axis == 0 else t[0]
            across = t[0] if axis == 0 else t[0] >> 2
            offset = offsets[0]
            for k in range(1, count):
                offset = jnp.where(c == k, offsets[k], offset)
            along = (along + offset) & 3
            across = (across + OTHER[part]) & 3
            block = along * SIDE + across if axis == 0 else across * SIDE + along
            return (m, 0, block)

        return pl.BlockSpec((1, tokens, TILE), index)

    def out_spec(k):
        def index(c, m, t):
            place = jnp.where(c == k, m, jnp.where(c < k, 0, mats - 1)) if count > 1 else m
            return (0, place, 0, 0)

        return pl.BlockSpec((SIDE, 1, TILE, TILE), index)

    out_type = jax.ShapeDtypeStruct((SIDE, mats, TILE, TILE), bf16)
    return pl.pallas_call(
        functools.partial(product_kernel, count),
        grid_spec=pltpu.PrefetchScalarGridSpec(
            num_scalar_prefetch=1,
            grid=(count, mats),
            in_specs=[block_spec(part) for part in range(SIDE)]
            + [pl.BlockSpec((tokens, 2 * TILE), lambda c, m, t: (0, axis))],
            out_specs=[out_spec(k) for k in range(count) for _ in (0, 1)],
        ),
        out_shape=[out_type] * (2 * count),
        compiler_params=pltpu.CompilerParams(vmem_limit_bytes=40 * 2**20),
        cost_estimate=pl.CostEstimate(
            flops=count * mats * 2 * 1024 * 1024 * 512,
            bytes_accessed=count * mats * 3 * 2**20,
            transcendentals=0,
        ),
    )(here, out_grads, out_grads, out_grads, out_grads, activations)


def shift_pairs(axis, step):
    pairs = []
    for x in range(SIDE):
        for z in range(SIDE):
            to = ((x + step) % SIDE, z) if axis == 0 else (x, (z + step) % SIDE)
            pairs.append((x * SIDE + z, to[0] * SIDE + to[1]))
    return pairs


def send(value, axis, step):
    return lax.ppermute(value, "col", shift_pairs(axis, step))


def after(value, *others):
    return lax.optimization_barrier((value,) + others)[0]


def add(*values):
    total = values[0].astype(f32)
    for value in values[1:]:
        total = total + value.astype(f32)
    return total


OTHER = (2, 1, 3, 0)
PARTS = (slice(0, 3), slice(3, 4))


def body(activations, out_grads, weights, row_prev, col_prev):
    mats = weights.shape[0]
    here = lax.axis_index("col").astype(jnp.int32).reshape(1)
    both = (0, 1)

    got1 = []
    for axis in both:
        low, high = products(here, out_grads, activations, axis, (2,))
        got1.append((send(low, axis, 1), send(high, axis, -1)))
    near = [products(here, out_grads, activations, axis, (1, 3)) for axis in both]
    got2, got3 = [], []
    for axis in both:
        low_next, high_next, low_last, high_last = near[axis]
        up, down = got1[axis]
        high_next, low_last, up, down = lax.optimization_barrier((high_next, low_last, up, down))
        got2.append((send(high_next, axis, 1), send(low_last, axis, -1)))
        plus = [add(low_next[s], up[s]).astype(bf16) for s in PARTS]
        minus = [add(high_last[s], down[s]).astype(bf16) for s in PARTS]
        first = (send(plus[0], axis, 1), send(minus[0], axis, -1))
        last = lax.optimization_barrier((plus[1], minus[1]) + first)
        got3.append((last[2:], (send(last[0], axis, 1), send(last[1], axis, -1))))
    own = []
    for axis in both:
        own.append(products(after(here, got1[1][0]), out_grads, activations, axis, (0,)))
    reduced = []
    for axis in both:
        for k in both:
            reduced.append(
                [
                    add(own[axis][k][s], got3[axis][n][k], got2[axis][1 - k][s])
                    for n, s in enumerate(PARTS)
                ]
            )
    got4 = []
    for axis in both:
        low = reduced[2 * axis][0].astype(bf16)
        high = reduced[2 * axis + 1][0].astype(bf16)
        plus = jnp.stack([low[0], high[1]])
        minus = jnp.stack([high[0], low[2]])
        got4.append((send(plus, 1 - axis, 1), send(minus, 1 - axis, -1)))
    pieces = []
    for axis in both:
        low, high = reduced[2 * axis], reduced[2 * axis + 1]
        up, down = got4[axis]
        plus = add(low[0][1].astype(bf16), up[0]).astype(bf16)
        minus = add(high[0][2].astype(bf16), down[0]).astype(bf16)
        up5, down5 = send(plus, 1 - axis, 1), send(minus, 1 - axis, -1)
        pieces.append(low[1][0] + add(up5, down[1]))
        pieces.append(high[1][0] + add(down5, up[1]))
    gradient = jnp.concatenate(pieces, axis=2)

    param_squares = jnp.sum(weights * weights, axis=(1, 2))
    pure = gradient * gradient
    square = pure + square_eps
    stage = jnp.concatenate([jnp.sum(square, axis=2).reshape(-1), param_squares])
    stage = lax.psum(stage, "row")
    row_sum = stage[: mats * TILE].reshape(mats, TILE)
    param_part = stage[mats * TILE :]
    row_new = decay_rate * row_prev + (1.0 - decay_rate) * row_sum / D
    col_part = jnp.sum(square, axis=1)
    mix_part = jnp.sum(pure * (1.0 / row_new)[:, :, None], axis=1)
    scalars = jnp.concatenate([jnp.sum(row_new, axis=1), param_part])
    payload = jnp.concatenate(
        [
            col_part.reshape(-1, 128),
            mix_part.reshape(-1, 128),
            jnp.pad(scalars, (0, 8 * 128 - 2 * mats)).reshape(8, 128),
        ]
    )
    gathered = lax.all_to_all(
        jnp.broadcast_to(payload[None], (SIDE * SIDE,) + payload.shape), "col", 0, 0
    )
    total = jnp.sum(gathered, axis=0)
    lines = mats * 1024 // 128
    col_sum = total[:lines].reshape(mats, 1024)
    mix_sum = total[lines : 2 * lines].reshape(mats, 1024)
    row_mean = total[2 * lines, :mats] / INNER
    param_totals = total[2 * lines, mats : 2 * mats]
    col_new = decay_rate * col_prev + (1.0 - decay_rate) * col_sum / INNER
    scaled_total = lax.psum(jnp.sum(mix_sum / col_new, axis=1), "row") * row_mean
    entry_count = INNER * D
    update_scale = jnp.sqrt(scaled_total / entry_count + 1e-06)
    param_scale = jnp.sqrt(param_totals / entry_count + 1e-06)
    shrink = jnp.sqrt(row_mean) / jnp.maximum(1.0, update_scale / clip_limit)
    row_factor = lax.rsqrt(row_new)
    col_factor = lax.rsqrt(col_new) * shrink[:, None]
    clipped = gradient * row_factor[:, :, None] * col_factor[:, None, :]
    updated = weights - (step_scale * param_scale)[:, None, None] * clipped
    return updated, clipped.astype(bf16), row_new, col_new, update_scale, param_scale


def solution(mesh):
    placed = (
        P(("section", "col"), "row"),
        P(None, ("section", "col"), None),
        P("section", "col", "row"),
        P("section", "col"),
        P("section", "row"),
    )
    return jax.shard_map(
        body,
        mesh=mesh,
        in_specs=placed,
        out_specs=(
            P("section", "col", "row"),
            P("section", "col", "row"),
            P("section", "col"),
            P("section", "row"),
            P("section"),
            P("section"),
        ),
        check_vma=False,
    )
```

```python
import functools

import jax
import jax.numpy as jnp
from jax import lax
from jax.experimental import pallas as pl
from jax.experimental.pallas import tpu as pltpu
from jax.sharding import PartitionSpec as P

D = 4096
INNER = 4096
SIDE = 4
TILE = 256

decay_rate = 1.0 - 100.0 ** (-0.8)
square_eps = 1e-30
step_scale = 0.01
clip_limit = 1.0
f32 = jnp.float32
bf16 = jnp.bfloat16


def chunk_kernel(near, here, d0, d1, d2, d3, x_ref, *targets):
    blocks = jnp.concatenate([d0[0], d1[0], d2[0], d3[0]], axis=1)
    term = lax.dot_general(
        blocks, x_ref[...], (((0,), (0,)), ((), ())), preferred_element_type=f32
    ).astype(bf16)

    def store(target, *columns):
        for part in range(SIDE):
            rows = slice(part * TILE, (part + 1) * TILE)
            if len(columns) == 1:
                target[part, 0] = term[rows, columns[0]]
            else:
                target[0, part, 0] = term[rows, columns[0]]
                target[1, part, 0] = term[rows, columns[1]]

    lower, upper = slice(0, TILE), slice(TILE, 2 * TILE)
    if near:
        pl.when(pl.program_id(1) == 0)(lambda: store(targets[0], upper, lower))
        pl.when(pl.program_id(1) == 1)(lambda: store(targets[1], lower, upper))
    else:
        store(targets[0], lower)
        store(targets[1], upper)


def feature_block(here, axis, offset, part):
    along = here >> 2 if axis == 0 else here
    across = here if axis == 0 else here >> 2
    along = (along + offset) & 3
    across = (across + OTHER[part]) & 3
    return along * SIDE + across if axis == 0 else across * SIDE + along


def chunk_products(here, out_grads, activations, axis, offsets):
    near = len(offsets) == 2
    mats, tokens, _ = out_grads.shape

    def block_spec(part):
        def index(m, c, t):
            offset = jnp.where(c == 0, offsets[0], offsets[1]) if near else offsets[0]
            return (m, 0, feature_block(t[0], axis, offset, part))

        return pl.BlockSpec((1, tokens, TILE), index)

    shape, block = (SIDE, mats, TILE, TILE), (SIDE, 1, TILE, TILE)
    out_spec = pl.BlockSpec(block, lambda m, c, t: (0, m, 0, 0))
    if near:
        shape, block = (2,) + shape, (2,) + block
        out_spec = pl.BlockSpec(block, lambda m, c, t: (0, 0, m, 0, 0))
    return pl.pallas_call(
        functools.partial(chunk_kernel, near),
        grid_spec=pltpu.PrefetchScalarGridSpec(
            num_scalar_prefetch=1,
            grid=(mats, len(offsets)),
            in_specs=[block_spec(part) for part in range(SIDE)]
            + [pl.BlockSpec((tokens, 2 * TILE), lambda m, c, t: (0, axis))],
            out_specs=[out_spec] * 2,
        ),
        out_shape=[jax.ShapeDtypeStruct(shape, bf16)] * 2,
        compiler_params=pltpu.CompilerParams(vmem_limit_bytes=40 * 2**20),
    )(here, out_grads, out_grads, out_grads, out_grads, activations)


def shift_pairs(axis, step):
    pairs = []
    for x in range(SIDE):
        for z in range(SIDE):
            to = ((x + step) % SIDE, z) if axis == 0 else (x, (z + step) % SIDE)
            pairs.append((x * SIDE + z, to[0] * SIDE + to[1]))
    return pairs


def send(value, axis, step):
    return lax.ppermute(value, "col", shift_pairs(axis, step))


def after(value, *others):
    return lax.optimization_barrier((value,) + others)[0]


def together(values):
    return lax.optimization_barrier(values)


def add(*values):
    total = values[0].astype(f32)
    for value in values[1:]:
        total = total + value.astype(f32)
    return total


OTHER = (2, 1, 3, 0)
ORDER = (1, 0)


def body(activations, out_grads, weights, row_prev, col_prev):
    mats = weights.shape[0]
    here = lax.axis_index("col").astype(jnp.int32).reshape(1)
    both = (0, 1)

    got1 = [None, None]
    for axis in ORDER:
        low, high = chunk_products(here, out_grads, activations, axis, (2,))
        got1[axis] = (send(low, axis, 1), send(high, axis, -1))
    near = together([chunk_products(here, out_grads, activations, axis, (1, -1)) for axis in both])
    got2, sent = [None, None], []
    for axis in ORDER:
        terms = [
            terms.at[1].set(add(terms[1], arrived).astype(bf16))
            for terms, arrived in zip(near[axis], got1[axis])
        ]
        got2[axis] = (send(terms[0], axis, 1), send(terms[1], axis, -1))
        sent += terms
    ready = after(here, *sent)
    own = [chunk_products(ready, out_grads, activations, axis, (0,)) for axis in both]
    reduced = []
    for axis in both:
        up, down = got2[axis]
        reduced.append(add(own[axis][0], up[1], down[0]))
        reduced.append(add(own[axis][1], down[1], up[0]))
    got4 = []
    for axis in both:
        low, high = reduced[2 * axis], reduced[2 * axis + 1]
        plus = jnp.stack([low[0], high[1]]).astype(bf16)
        minus = jnp.stack([high[0], low[2]]).astype(bf16)
        got4.append((send(plus, 1 - axis, 1), send(minus, 1 - axis, -1)))
    pieces = []
    for axis in both:
        low, high = reduced[2 * axis], reduced[2 * axis + 1]
        up, down = got4[axis]
        plus = add(low[1], up[0]).astype(bf16)
        minus = add(high[2], down[0]).astype(bf16)
        up5, down5 = send(plus, 1 - axis, 1), send(minus, 1 - axis, -1)
        pieces.append(add(low[3], up5, down[1]))
        pieces.append(add(high[3], down5, up[1]))
    gradient = jnp.concatenate(pieces, axis=2)

    param_squares = jnp.sum(weights * weights, axis=(1, 2))
    pure = gradient * gradient
    square = pure + square_eps
    stage = jnp.concatenate([jnp.sum(square, axis=2).reshape(-1), param_squares])
    stage = lax.psum(stage, "row")
    row_sum = stage[: mats * TILE].reshape(mats, TILE)
    param_part = stage[mats * TILE :]
    row_new = decay_rate * row_prev + (1.0 - decay_rate) * row_sum / D
    col_part = jnp.sum(square, axis=1)
    base = gradient * lax.rsqrt(row_new)[:, :, None]
    mix_part = jnp.sum(base * base, axis=1)
    scalars = jnp.concatenate([jnp.sum(row_new, axis=1), param_part])
    payload = jnp.concatenate(
        [
            col_part.reshape(-1, 128),
            mix_part.reshape(-1, 128),
            jnp.pad(scalars, (0, 8 * 128 - 2 * mats)).reshape(8, 128),
        ]
    )
    gathered = lax.all_to_all(
        jnp.broadcast_to(payload[None], (SIDE * SIDE,) + payload.shape), "col", 0, 0
    )
    total = jnp.sum(gathered, axis=0)
    lines = mats * 1024 // 128
    col_sum = total[:lines].reshape(mats, 1024)
    mix_sum = total[lines : 2 * lines].reshape(mats, 1024)
    row_mean = total[2 * lines, :mats] / INNER
    param_totals = total[2 * lines, mats : 2 * mats]
    col_new = decay_rate * col_prev + (1.0 - decay_rate) * col_sum / INNER
    scaled_total = lax.psum(jnp.sum(mix_sum / col_new, axis=1), "row") * row_mean
    entry_count = INNER * D
    update_scale = jnp.sqrt(scaled_total / entry_count + 1e-06)
    param_scale = jnp.sqrt(param_totals / entry_count + 1e-06)
    shrink = jnp.sqrt(row_mean) / jnp.maximum(1.0, update_scale / clip_limit)
    col_factor = lax.rsqrt(col_new) * shrink[:, None]
    clipped = base * col_factor[:, None, :]
    updated = weights - (step_scale * param_scale)[:, None, None] * clipped
    direction = clipped.astype(bf16)
    return updated, direction, row_new, col_new, update_scale, param_scale


def solution(mesh):
    placed = (
        P(("section", "col"), "row"),
        P(None, ("section", "col"), None),
        P("section", "col", "row"),
        P("section", "col"),
        P("section", "row"),
    )
    return jax.shard_map(
        body,
        mesh=mesh,
        in_specs=placed,
        out_specs=(
            P("section", "col", "row"),
            P("section", "col", "row"),
            P("section", "col"),
            P("section", "row"),
            P("section"),
            P("section"),
        ),
        check_vma=False,
    )
```

```python
import functools

import jax
import jax.numpy as jnp
from jax import lax
from jax.experimental import pallas as pl
from jax.experimental.pallas import tpu as pltpu
from jax.sharding import PartitionSpec as P

D = 4096
INNER = 4096
SIDE = 4
TILE = 256

decay_rate = 1.0 - 100.0 ** (-0.8)
square_eps = 1e-30
step_scale = 0.01
clip_limit = 1.0
f32 = jnp.float32
bf16 = jnp.bfloat16


def chunk_kernel(near, here, d0, d1, d2, d3, x_ref, *targets):
    blocks = jnp.concatenate([d0[0], d1[0], d2[0], d3[0]], axis=1)
    term = lax.dot_general(
        blocks, x_ref[...], (((0,), (0,)), ((), ())), preferred_element_type=f32
    ).astype(bf16)

    def store(target, *columns):
        for part in range(SIDE):
            rows = slice(part * TILE, (part + 1) * TILE)
            if len(columns) == 1:
                target[part, 0] = term[rows, columns[0]]
            else:
                target[0, part, 0] = term[rows, columns[0]]
                target[1, part, 0] = term[rows, columns[1]]

    lower, upper = slice(0, TILE), slice(TILE, 2 * TILE)
    if near:
        pl.when(pl.program_id(1) == 0)(lambda: store(targets[0], upper, lower))
        pl.when(pl.program_id(1) == 1)(lambda: store(targets[1], lower, upper))
    else:
        store(targets[0], lower)
        store(targets[1], upper)


def feature_block(table, axis, offset, part):
    along = (table[axis] + offset) & 3
    across = (table[1 - axis] + OTHER[part]) & 3
    return along * table[2 + axis] + across * table[3 - axis]


def chunk_products(here, out_grads, activations, axis, offsets):
    near = len(offsets) == 2
    mats, tokens, _ = out_grads.shape

    def block_spec(part):
        def index(m, c, t):
            offset = jnp.where(c == 0, offsets[0], offsets[1]) if near else offsets[0]
            return (m, 0, feature_block(t, axis, offset, part))

        return pl.BlockSpec((1, tokens, TILE), index)

    shape, block = (SIDE, mats, TILE, TILE), (SIDE, 1, TILE, TILE)
    out_spec = pl.BlockSpec(block, lambda m, c, t: (0, m, 0, 0))
    if near:
        shape, block = (2,) + shape, (2,) + block
        out_spec = pl.BlockSpec(block, lambda m, c, t: (0, 0, m, 0, 0))
    return pl.pallas_call(
        functools.partial(chunk_kernel, near),
        grid_spec=pltpu.PrefetchScalarGridSpec(
            num_scalar_prefetch=1,
            grid=(mats, len(offsets)),
            in_specs=[block_spec(part) for part in range(SIDE)]
            + [pl.BlockSpec((tokens, 2 * TILE), lambda m, c, t: (0, axis))],
            out_specs=[out_spec] * 2,
        ),
        out_shape=[jax.ShapeDtypeStruct(shape, bf16)] * 2,
        compiler_params=pltpu.CompilerParams(vmem_limit_bytes=40 * 2**20),
    )(here, out_grads, out_grads, out_grads, out_grads, activations)


def shift_pairs(axis, step):
    pairs = []
    for section in (0, 1):
        for x in range(SIDE):
            for z in range(SIDE):
                along_x = axis == section
                to = ((x + step) % SIDE, z) if along_x else (x, (z + step) % SIDE)
                base = section * SIDE * SIDE
                pairs.append((base + x * SIDE + z, base + to[0] * SIDE + to[1]))
    return pairs


def send(value, axis, step):
    return lax.ppermute(value, ("section", "col"), shift_pairs(axis, step))


def after(value, *others):
    return lax.optimization_barrier((value,) + others)[0]


def add(*values):
    total = values[0].astype(f32)
    for value in values[1:]:
        total = total + value.astype(f32)
    return total


OTHER = (2, 1, 3, 0)
ORDER = (0, 1)


def body(activations, out_grads, weights, row_prev, col_prev):
    mats = weights.shape[0]
    section = lax.axis_index("section").astype(jnp.int32)
    col = lax.axis_index("col").astype(jnp.int32)
    x, z, stride = col >> 2, col & 3, jnp.where(section == 0, SIDE, 1)
    here = jnp.stack(
        [jnp.where(section == 0, x, z), jnp.where(section == 0, z, x), stride, SIDE + 1 - stride]
    )
    both = (0, 1)

    got1 = [None, None]
    for axis in ORDER:
        low, high = chunk_products(here, out_grads, activations, axis, (2,))
        got1[axis] = (send(low, axis, 1), send(high, axis, -1))
    near = [chunk_products(here, out_grads, activations, axis, (1, -1)) for axis in both]
    got2, sent = [None, None], []
    for axis in ORDER:
        terms = [
            terms.at[1].set(add(terms[1], arrived).astype(bf16))
            for terms, arrived in zip(near[axis], got1[axis])
        ]
        got2[axis] = (send(terms[0], axis, 1), send(terms[1], axis, -1))
        sent += terms
    ready = after(here, *sent)
    own = [chunk_products(ready, out_grads, activations, axis, (0,)) for axis in both]
    reduced = []
    for axis in both:
        up, down = got2[axis]
        reduced.append(add(own[axis][0], up[1], down[0]))
        reduced.append(add(own[axis][1], down[1], up[0]))
    got4 = []
    for axis in both:
        low, high = reduced[2 * axis], reduced[2 * axis + 1]
        plus = jnp.stack([low[0], high[1]]).astype(bf16)
        minus = jnp.stack([high[0], low[2]]).astype(bf16)
        got4.append((send(plus, 1 - axis, 1), send(minus, 1 - axis, -1)))
    pieces = []
    for axis in both:
        low, high = reduced[2 * axis], reduced[2 * axis + 1]
        up, down = got4[axis]
        plus = add(low[1], up[0]).astype(bf16)
        minus = add(high[2], down[0]).astype(bf16)
        up5, down5 = send(plus, 1 - axis, 1), send(minus, 1 - axis, -1)
        pieces.append(add(low[3], up5, down[1]))
        pieces.append(add(high[3], down5, up[1]))
    gradient = jnp.concatenate(pieces, axis=2)

    param_squares = jnp.sum(weights * weights, axis=(1, 2))
    pure = gradient * gradient
    square = pure + square_eps
    stage = jnp.concatenate([jnp.sum(square, axis=2).reshape(-1), param_squares])
    stage = lax.psum(stage, "row")
    row_sum = stage[: mats * TILE].reshape(mats, TILE)
    param_part = stage[mats * TILE :]
    row_new = decay_rate * row_prev + (1.0 - decay_rate) * row_sum / D
    col_part = jnp.sum(square, axis=1)
    base = gradient * lax.rsqrt(row_new)[:, :, None]
    mix_part = jnp.sum(base * base, axis=1)
    scalars = jnp.concatenate([jnp.sum(row_new, axis=1), param_part])
    payload = jnp.concatenate(
        [
            col_part.reshape(-1, 128),
            mix_part.reshape(-1, 128),
            jnp.pad(scalars, (0, 8 * 128 - 2 * mats)).reshape(8, 128),
        ]
    )
    gathered = lax.all_to_all(
        jnp.broadcast_to(payload[None], (SIDE * SIDE,) + payload.shape), "col", 0, 0
    )
    total = jnp.sum(gathered, axis=0)
    lines = mats * 1024 // 128
    col_sum = total[:lines].reshape(mats, 1024)
    mix_sum = total[lines : 2 * lines].reshape(mats, 1024)
    row_mean = total[2 * lines, :mats] / INNER
    param_totals = total[2 * lines, mats : 2 * mats]
    col_new = decay_rate * col_prev + (1.0 - decay_rate) * col_sum / INNER
    scaled_total = lax.psum(jnp.sum(mix_sum / col_new, axis=1), "row") * row_mean
    entry_count = INNER * D
    update_scale = jnp.sqrt(scaled_total / entry_count + 1e-06)
    param_scale = jnp.sqrt(param_totals / entry_count + 1e-06)
    shrink = jnp.sqrt(row_mean) / jnp.maximum(1.0, update_scale / clip_limit)
    col_factor = lax.rsqrt(col_new) * shrink[:, None]
    clipped = base * col_factor[:, None, :]
    updated = weights - (step_scale * param_scale)[:, None, None] * clipped
    direction = clipped.astype(bf16)
    return updated, direction, row_new, col_new, update_scale, param_scale


def solution(mesh):
    placed = (
        P(("section", "col"), "row"),
        P(None, ("section", "col"), None),
        P("section", "col", "row"),
        P("section", "col"),
        P("section", "row"),
    )
    return jax.shard_map(
        body,
        mesh=mesh,
        in_specs=placed,
        out_specs=(
            P("section", "col", "row"),
            P("section", "col", "row"),
            P("section", "col"),
            P("section", "row"),
            P("section"),
            P("section"),
        ),
        check_vma=False,
    )
```
